32 devices in a mesh: ctx: 16 (over z, y, x), tp: 2 (over core).
Axes of the slice: x: 2, y: 2, z: 4, core: 2. Of those that a mesh axis runs over, the one named last changes fastest.
Arguments:
- features: bfloat16 [3, 1024, 8192], P(None, 'ctx', 'tp'), may hold values from -6 to 6
- short_weight: float32 [3, 3, 8192], P(None, None, 'tp'), may hold values from -3 to 3
- decay_rate: float32 [512, 16], P('tp'), may hold values from 0.00048828125 to 0.03
- residue: float32 [512, 16], P('tp'), may hold values from -3 to 3
- skip_gain: float32 [8192], P('tp'), may hold values from -1 to 1
- out_weight: bfloat16 [8192, 4096], P('tp', 'ctx'), may hold values from -0.09375 to 0.09375
Outputs:
- mixed_out: bfloat16 [1024, 4096], P('ctx', 'tp')
The draws below stay inside these ranges and needn't reach their ends.
All inputs are finite; a program needn't handle non-finite values.
Results may differ from the reference program's by a relative error of at most 0.006.
Values may be sent and summed in bfloat16 or wider, within the bound.
A program may use at most 128 MiB of HBM per device.

```python
import math
import jax
import jax.numpy as jnp
from jax import lax

D = 8192
D_OUT = 4096
G = 512
S = 16
KS = 3
TOK_DEV = 64
SEQ = 1024


def with_spikes(drawn, key, source, target, parts, factor):
    owner, partner = [(jnp.arange(drawn.shape[axis_at]) // (drawn.shape[axis_at] // parts)).reshape([-1 if axis == axis_at else 1 for axis in range(drawn.ndim)]) for axis_at in (source, target)]
    chosen = jax.random.permutation(key, parts)[partner]
    strong = (owner == chosen) | (owner == (partner + parts // 2) % parts)
    return jnp.where(strong, factor * drawn, drawn)


def steps_of(key, dims, cuts, least, largest):
    gain, own = 1.0, jax.random.fold_in(key, 6)
    for axis_at, parts in cuts:
        steps = jnp.exp(jax.random.uniform(jax.random.fold_in(own, axis_at), (parts,), jnp.float32, least / len(cuts), largest / len(cuts)))
        gain = gain * jnp.repeat(steps, dims[axis_at] // parts).reshape([-1 if axis == axis_at else 1 for axis in range(len(dims))])
    return gain


def gaussian(rng, shape, scale, bound, split=(), kind=jnp.bfloat16):
    entries = scale * jax.random.normal(rng, shape, jnp.float32)
    if split:
        entries = entries * steps_of(rng, shape, split, -0.22, 0.18)
    return jnp.clip(entries, -bound, bound).astype(kind)


def bell_draw_with(rng, extent, scale, bound, shards, heavy, held_as=jnp.bfloat16):
    drawn = scale * jax.random.normal(rng, extent, jnp.float32)
    if shards:
        drawn = drawn * steps_of(rng, extent, shards, -0.22, 0.18)
    return jnp.clip(with_spikes(drawn, jax.random.fold_in(rng, 3), *heavy), -bound, bound).astype(held_as)


def setup_inputs(seed: int = 0) -> dict:
    key_of = jax.random.split(jax.random.key(seed), 7)
    features = gaussian(key_of[0], (3, SEQ, D), 1.0, 6.0, ((1, 16), (2, 2)))
    short_weight = gaussian(key_of[1], (3, KS, D), 0.6, 3.0, ((2, 2),), jnp.float32)
    decay_rate = jnp.clip(jnp.exp(math.log(0.03) - 4.118061 * jax.random.uniform(key_of[2], (G, S), jnp.float32) ** steps_of(key_of[2], (G, S), ((0, 2),), -0.2, 0.2)), 0.00048828125, 0.03)
    residue = gaussian(key_of[3], (G, S), 0.5, 3.0, ((0, 2),), jnp.float32)
    skip_gain = jnp.clip(jax.random.uniform(key_of[4], (D,), jnp.float32, -1.0, 1.0) * steps_of(key_of[4], (D,), ((0, 2),), -0.4, 0.0), -1.0, 1.0)
    out_weight = bell_draw_with(key_of[5], (D, D_OUT), D ** -0.5, 0.09375, ((0, 2), (1, 16)), (0, 1, 16, 2.0))
    return {"features": features, "short_weight": short_weight, "decay_rate": decay_rate, "residue": residue, "skip_gain": skip_gain, "out_weight": out_weight}


def reference(features, short_weight, decay_rate, residue, skip_gain, out_weight):
    hi = lax.Precision.HIGHEST
    xs = features.astype(jnp.float32)
    conv = jnp.zeros(xs.shape, jnp.float32)
    for j in range(KS):
        moved = jnp.pad(xs, ((0, 0), (j, 0), (0, 0)))[:, :SEQ, :]
        conv = conv + short_weight[:, j][:, None, :] * moved
    q_lane = conv[0]
    gated = (conv[1] * conv[2]).astype(jnp.bfloat16)
    coef = residue * jnp.sqrt(-jnp.expm1(-2.0 * decay_rate))
    lags = jnp.arange(TOK_DEV, dtype=jnp.float32)
    near_filter = lax.optimization_barrier(jnp.sum(coef[:, :, None] * jnp.exp(-decay_rate[:, :, None] * lags[None, None, :]), axis=1)).astype(jnp.bfloat16)
    rows = jnp.arange(TOK_DEV, dtype=jnp.int32)
    offset = rows[:, None] - rows[None, :]
    toeplitz = jnp.where(offset[None] >= 0, near_filter[:, jnp.clip(offset, 0, TOK_DEV - 1)], jnp.zeros((), jnp.bfloat16)).astype(jnp.float32)
    far_basis = coef[None] * jnp.exp(-decay_rate[None] * (lags + 1.0)[:, None, None])
    end_basis = jnp.exp(-decay_rate[None] * (TOK_DEV - 1.0 - lags)[:, None, None])
    block_decay = jnp.exp(-decay_rate * TOK_DEV)
    width = D // G
    blocks = gated.astype(jnp.float32).reshape(SEQ // TOK_DEV, TOK_DEV, G, width)

    def step(state, block):
        near = jnp.einsum('gts,sgw->tgw', toeplitz, block, precision=hi)
        far = jnp.einsum('tgs,gws->tgw', far_basis, state, precision=hi)
        state = block_decay[:, None, :] * state + jnp.einsum('tgs,tgw->gws', end_basis, block, precision=hi)
        return (state, near + far)
    start = jnp.zeros((G, width, S), jnp.float32)
    _, outs = lax.scan(step, start, blocks)
    filtered = outs.reshape(SEQ, D) + skip_gain[None, :] * gated.astype(jnp.float32)
    mixed = (q_lane * filtered).astype(jnp.bfloat16)
    return jnp.dot(mixed, out_weight, preferred_element_type=jnp.float32).astype(jnp.bfloat16)
```

```python
import jax
import jax.numpy as jnp
from jax import lax
from jax.experimental import pallas as pl
from jax.experimental.pallas import tpu as pltpu
from jax.sharding import PartitionSpec as P

LANES = 128


def modal_sum(decay, weight, rows, shift):
    modes = decay.shape[0]
    lag = lax.broadcasted_iota(jnp.int32, (8, LANES), 0).astype(jnp.float32) + shift
    total = [jnp.zeros((8, LANES), jnp.float32) for _ in range(rows // 8)]
    for s in range(modes):
        rate = decay[s : s + 1]
        power = weight[s : s + 1] * jnp.exp(-rate * lag)
        stride = jnp.exp(-8.0 * rate)
        for b in range(rows // 8):
            total[b] = total[b] + power
            if b + 1 < rows // 8:
                power = power * stride
    return total


def front_kernel(x_ref, rim_ref, w_ref, decay_ref, coef_ref, skip_ref, q_ref, base_ref, state_ref, ext, filt, gate):
    rows = x_ref.shape[1]
    taps = w_ref.shape[1]
    modes = decay_ref.shape[0]
    nb = rows // 8

    def tile(i, carry):
        at = pl.ds(pl.multiple_of(i * LANES, LANES), LANES)
        conv = []
        for lane in range(3):
            ext[lane, 0:8] = rim_ref[lane, :, at].astype(jnp.float32)
            ext[lane, 8 : 8 + rows] = x_ref[lane, :, at].astype(jnp.float32)
            acc = jnp.zeros((rows, LANES), jnp.float32)
            for j in range(taps):
                acc = acc + w_ref[lane, j : j + 1, at] * ext[lane, 8 - j : 8 - j + rows]
            conv.append(acc)
        q_ref[:, at] = conv[0]
        gated = (conv[1] * conv[2]).astype(jnp.bfloat16).astype(jnp.float32)
        gate[...] = gated
        decay = decay_ref[:, at]
        coef = coef_ref[:, at]
        filt[0:8] = jnp.zeros((8, LANES), jnp.float32)
        for b, part in enumerate(modal_sum(decay, coef, rows, 0.0)):
            filt[8 + 8 * b : 16 + 8 * b] = part.astype(jnp.bfloat16).astype(jnp.float32)
        skip = skip_ref[:, at]
        out = [skip * gated[8 * b : 8 * b + 8] for b in range(nb)]
        for t in range(rows):
            row = jnp.broadcast_to(gate[t : t + 1], (8, LANES))
            for b in range(t // 8, nb):
                start = 8 + 8 * b - t
                out[b] = out[b] + filt[start : start + 8] * row
        for b in range(nb):
            base_ref[8 * b : 8 * b + 8, at] = out[b]
        left = 7.0 - lax.broadcasted_iota(jnp.int32, (8, LANES), 0).astype(jnp.float32)
        ends = []
        for s in range(modes):
            rate = decay[s : s + 1]
            stride = jnp.exp(-8.0 * rate)
            acc = gated[0:8]
            for b in range(1, nb):
                acc = acc * stride + gated[8 * b : 8 * b + 8]
            ends.append(jnp.sum(acc * jnp.exp(-rate * left), axis=0, keepdims=True))
        state_ref[:, at] = jnp.concatenate(ends, axis=0)
        return carry

    lax.fori_loop(0, x_ref.shape[2] // LANES, tile, 0)


def back_kernel(q_ref, base_ref, state_ref, decay_ref, coef_ref, mixed_ref):
    rows = q_ref.shape[0]

    def tile(i, carry):
        at = pl.ds(pl.multiple_of(i * LANES, LANES), LANES)
        far = modal_sum(decay_ref[:, at], coef_ref[:, at] * state_ref[:, at], rows, 1.0)
        whole = jnp.concatenate(far, axis=0) + base_ref[:, at]
        mixed_ref[:, at] = (q_ref[:, at] * whole).astype(jnp.bfloat16)
        return carry

    lax.fori_loop(0, q_ref.shape[1] // LANES, tile, 0)


def per_device(features, short_weight, decay_rate, residue, skip_gain, out_weight):
    lanes, rows, chans = features.shape
    groups, modes = decay_rate.shape
    width = chans // groups
    taps = short_weight.shape[1]
    count = lax.axis_size("ctx")
    tps = lax.axis_size("tp")
    me = lax.axis_index("ctx")
    cb = min(chans, 1024)
    pairs = [(i, i + 1) for i in range(count - 1)]
    rim = lax.ppermute(features[:, rows - (taps - 1) :, :], "ctx", pairs)
    rim = jnp.pad(rim, ((0, 0), (8 - (taps - 1), 0), (0, 0)))
    coef = residue * jnp.sqrt(-jnp.expm1(-2.0 * decay_rate))
    spread = (
        lax.broadcasted_iota(jnp.int32, (groups, chans), 1) // width
        == lax.broadcasted_iota(jnp.int32, (groups, chans), 0)
    ).astype(jnp.float32)
    both = jnp.concatenate([decay_rate, coef], axis=1)
    wide = jnp.einsum("gs,gc->sc", both, spread, precision=lax.Precision.HIGHEST)
    decay_wide, coef_wide = wide[:modes], wide[modes:]
    f32 = jnp.float32
    grid = (chans // cb,)
    plane = pl.BlockSpec((rows, cb), lambda i: (0, i))
    modal = pl.BlockSpec((modes, cb), lambda i: (0, i))
    q, base, own = pl.pallas_call(
        front_kernel,
        grid=grid,
        in_specs=[
            pl.BlockSpec((lanes, rows, cb), lambda i: (0, 0, i)),
            pl.BlockSpec((lanes, 8, cb), lambda i: (0, 0, i)),
            pl.BlockSpec((lanes, taps, cb), lambda i: (0, 0, i)),
            modal,
            modal,
            pl.BlockSpec((1, cb), lambda i: (0, i)),
        ],
        out_specs=[plane, plane, modal],
        out_shape=[
            jax.ShapeDtypeStruct((rows, chans), f32),
            jax.ShapeDtypeStruct((rows, chans), f32),
            jax.ShapeDtypeStruct((modes, chans), f32),
        ],
        scratch_shapes=[
            pltpu.VMEM((lanes, rows + 8, LANES), f32),
            pltpu.VMEM((rows + 8, LANES), f32),
            pltpu.VMEM((rows, LANES), f32),
        ],
        name="front",
    )(features, rim, short_weight, decay_wide, coef_wide, skip_gain[None])
    share = chans // count
    pieces = lax.all_to_all(own, "ctx", split_axis=1, concat_axis=0, tiled=True)
    mine = lax.dynamic_slice_in_dim(decay_wide, me * share, share, axis=1)
    block_decay = jnp.exp(-mine * rows)
    running = jnp.zeros((modes, share), f32)
    before = []
    for b in range(count):
        before.append(running)
        running = running * block_decay + pieces[b * modes : (b + 1) * modes]
    incoming = lax.all_to_all(
        jnp.concatenate(before, axis=0), "ctx", split_axis=0, concat_axis=1, tiled=True
    )
    mixed = pl.pallas_call(
        back_kernel,
        grid=grid,
        in_specs=[plane, plane, modal, modal, modal],
        out_specs=plane,
        out_shape=jax.ShapeDtypeStruct((rows, chans), jnp.bfloat16),
        name="back",
    )(q, base, incoming, decay_wide, coef_wide)
    every = lax.all_gather(mixed, "ctx", axis=0, tiled=True)
    partial_out = jnp.dot(every, out_weight, preferred_element_type=f32)
    cols = out_weight.shape[1]
    sums = lax.psum_scatter(partial_out, "tp", scatter_dimension=1, tiled=True).astype(jnp.bfloat16)
    turned = lax.all_to_all(sums, "ctx", split_axis=0, concat_axis=1, tiled=True)
    part = cols // tps
    swapped = lax.all_to_all(
        turned.reshape(rows, count * part), "tp", split_axis=1, concat_axis=0, tiled=True
    )
    swapped = swapped.reshape(tps, rows, count // tps, part)
    return swapped.transpose(1, 2, 0, 3).reshape(rows, count // tps * cols)


def solution(mesh):
    placed = (
        P(None, "ctx", "tp"),
        P(None, None, "tp"),
        P("tp", None),
        P("tp", None),
        P("tp"),
        P("tp", "ctx"),
    )
    return jax.shard_map(
        per_device, mesh=mesh, in_specs=placed, out_specs=P("ctx", "tp"), check_vma=False
    )
```

```python
import jax
import jax.numpy as jnp
from jax import lax
from jax.experimental import pallas as pl
from jax.experimental.pallas import tpu as pltpu
from jax.sharding import PartitionSpec as P

LANES = 128


def modal_sum(decay, weight, rows, shift):
    modes = decay.shape[0]
    lag = lax.broadcasted_iota(jnp.int32, (8, LANES), 0).astype(jnp.float32) + shift
    total = [jnp.zeros((8, LANES), jnp.float32) for _ in range(rows // 8)]
    for s in range(modes):
        rate = decay[s : s + 1]
        power = weight[s : s + 1] * jnp.exp(-rate * lag)
        stride = jnp.exp(-8.0 * rate)
        for b in range(rows // 8):
            total[b] = total[b] + power
            if b + 1 < rows // 8:
                power = power * stride
    return total


def front_kernel(x_ref, rim_ref, w_ref, decay_ref, coef_ref, skip_ref, q_ref, base_ref, state_ref, ext, filt, gate):
    rows = x_ref.shape[1]
    taps = w_ref.shape[1]
    modes = decay_ref.shape[0]
    nb = rows // 8

    def tile(i, carry):
        at = pl.ds(pl.multiple_of(i * LANES, LANES), LANES)
        conv = []
        for lane in range(3):
            ext[lane, 0:8] = rim_ref[lane, :, at].astype(jnp.float32)
            ext[lane, 8 : 8 + rows] = x_ref[lane, :, at].astype(jnp.float32)
            acc = jnp.zeros((rows, LANES), jnp.float32)
            for j in range(taps):
                acc = acc + w_ref[lane, j : j + 1, at] * ext[lane, 8 - j : 8 - j + rows]
            conv.append(acc)
        q_ref[:, at] = conv[0]
        gated = (conv[1] * conv[2]).astype(jnp.bfloat16).astype(jnp.float32)
        gate[...] = gated
        decay = decay_ref[:, at]
        coef = coef_ref[:, at]
        filt[0:8] = jnp.zeros((8, LANES), jnp.float32)
        for b, part in enumerate(modal_sum(decay, coef, rows, 0.0)):
            filt[8 + 8 * b : 16 + 8 * b] = part.astype(jnp.bfloat16).astype(jnp.float32)
        skip = skip_ref[:, at]
        out = [skip * gated[8 * b : 8 * b + 8] for b in range(nb)]
        for t in range(rows):
            row = jnp.broadcast_to(gate[t : t + 1], (8, LANES))
            for b in range(t // 8, nb):
                start = 8 + 8 * b - t
                out[b] = out[b] + filt[start : start + 8] * row
        for b in range(nb):
            base_ref[8 * b : 8 * b + 8, at] = out[b]
        left = 7.0 - lax.broadcasted_iota(jnp.int32, (8, LANES), 0).astype(jnp.float32)
        ends = []
        for s in range(modes):
            rate = decay[s : s + 1]
            stride = jnp.exp(-8.0 * rate)
            acc = gated[0:8]
            for b in range(1, nb):
                acc = acc * stride + gated[8 * b : 8 * b + 8]
            ends.append(jnp.sum(acc * jnp.exp(-rate * left), axis=0, keepdims=True))
        state_ref[:, at] = jnp.concatenate(ends, axis=0)
        return carry

    lax.fori_loop(0, x_ref.shape[2] // LANES, tile, 0)


def back_kernel(q_ref, base_ref, state_ref, decay_ref, coef_ref, mixed_ref):
    rows = q_ref.shape[0]

    def tile(i, carry):
        at = pl.ds(pl.multiple_of(i * LANES, LANES), LANES)
        far = modal_sum(decay_ref[:, at], coef_ref[:, at] * state_ref[:, at], rows, 1.0)
        whole = jnp.concatenate(far, axis=0) + base_ref[:, at]
        mixed_ref[:, at] = (q_ref[:, at] * whole).astype(jnp.bfloat16)
        return carry

    lax.fori_loop(0, q_ref.shape[1] // LANES, tile, 0)


def finish_kernel(
    q_ref, base_ref, state_ref, decay_ref, coef_ref, own_ref, pair_ref, out_ref,
    blocks, result, other, packed,
    up_sem, down_sem, z_sem, ysend_sem, yrecv_sem, psend_sem, precv_sem, osend_sem, orecv_sem,
):
    rows = q_ref.shape[0]
    c, p = lax.axis_index("ctx"), lax.axis_index("tp")
    x, y, z = c % 2, (c // 2) % 2, c // 4
    depth = blocks.shape[0] // 2
    mesh_ids = pl.DeviceIdType.MESH
    barrier = pltpu.get_barrier_semaphore()
    for far_z in range(depth):
        for far_y in range(2):
            for far_p in range(2):
                spot = far_z * 4 + far_y * 2 + x

                @pl.when(jnp.logical_or(spot != c, p != far_p))
                def _():
                    pl.semaphore_signal(
                        barrier, inc=1, device_id=(spot, far_p), device_id_type=mesh_ids
                    )

    here = z * 2 + y

    def tile(i, carry):
        at = pl.ds(pl.multiple_of(i * LANES, LANES), LANES)
        far = modal_sum(decay_ref[:, at], coef_ref[:, at] * state_ref[:, at], rows, 1.0)
        whole = jnp.concatenate(far, axis=0) + base_ref[:, at]
        blocks[here, :, at] = (q_ref[:, at] * whole).astype(jnp.bfloat16)
        return carry

    lax.fori_loop(0, q_ref.shape[1] // LANES, tile, 0)
    pl.semaphore_wait(barrier, depth * 4 - 1)

    def along_z(level, step, sems, k):
        slot = level * 2 + y
        return pltpu.make_async_remote_copy(
            blocks.at[slot], blocks.at[slot], sems.at[k], z_sem.at[level],
            device_id=(c + 4 * step, p), device_id_type=mesh_ids,
        )

    def along_y(level):
        slot = level * 2 + y
        return pltpu.make_async_remote_copy(
            blocks.at[slot], blocks.at[slot], ysend_sem.at[level], yrecv_sem.at[level],
            device_id=(c + 2 - 4 * y, p), device_id_type=mesh_ids,
        )

    def to_core(level):
        return pltpu.make_async_remote_copy(
            result.at[level, 1 - p], other.at[level], psend_sem.at[level], precv_sem.at[level],
            device_id=(c, 1 - p), device_id_type=mesh_ids,
        )

    chunk = (c % 8) // 2 * 2 + p
    side = z // 2

    def to_owner(level, far_y):
        return pltpu.make_async_remote_copy(
            packed.at[level, far_y], out_ref.at[chunk], osend_sem.at[level, far_y], orecv_sem.at[chunk],
            device_id=(level * 4 + far_y * 2 + x, side), device_id_type=mesh_ids,
        )

    def multiply(level):
        pltpu.make_async_copy(blocks.at[level * 2 + 1 - y], blocks.at[level * 2 + 1 - y], yrecv_sem.at[level]).wait()
        lhs = blocks[pl.ds(level * 2, 2)].reshape(2 * rows, blocks.shape[2])
        result[level, x] = jnp.dot(lhs, own_ref[...], preferred_element_type=jnp.float32)
        result[level, 1 - x] = jnp.dot(lhs, pair_ref[...], preferred_element_type=jnp.float32)
        to_core(level).start()

    def deliver(level):
        to_core(level).wait_recv()
        total = result[level, p] + other[level]
        packed[level] = total.astype(jnp.bfloat16).reshape(2, rows, total.shape[1])
        for far_y in range(2):
            mine = jnp.logical_and(jnp.logical_and(level == z, far_y == y), side == p)

            @pl.when(mine)
            def _():
                out_ref[chunk] = packed[level, far_y]

            @pl.when(jnp.logical_not(mine))
            def _():
                to_owner(level, far_y).start()

    def both(k, act):
        @pl.when(z - k >= 0)
        def _():
            act(z - k, 1)

        if k:

            @pl.when(z + k < depth)
            def _():
                act(z + k, -1)

    can_up, can_down = z + 1 < depth, z >= 1

    def forward(level, step, k):
        if k + 1 < depth:
            if step > 0 or k == 0:

                @pl.when(can_up)
                def _():
                    along_z(level, 1, up_sem, k).start()

            if step < 0 or k == 0:

                @pl.when(can_down)
                def _():
                    along_z(level, -1, down_sem, k).start()

        along_y(level).start()

    def arrive(k):
        def act(level, step):
            pltpu.make_async_copy(blocks.at[level * 2 + y], blocks.at[level * 2 + y], z_sem.at[level]).wait()
            forward(level, step, k)

        return act

    forward(z, 1, 0)
    for k in range(1, depth):
        both(k, arrive(k))
        both(k - 1, lambda level, step: multiply(level))
        if k >= 2:
            both(k - 2, lambda level, step: deliver(level))
    both(depth - 1, lambda level, step: multiply(level))
    both(depth - 2, lambda level, step: deliver(level))
    both(depth - 1, lambda level, step: deliver(level))

    for level in range(depth):
        along_y(level).wait_send()
        to_core(level).wait_send()
        for far_y in range(2):
            mine = jnp.logical_and(jnp.logical_and(level == z, far_y == y), side == p)

            @pl.when(jnp.logical_not(mine))
            def _():
                to_owner(level, far_y).wait_send()

    for k in range(depth - 1):

        @pl.when(jnp.logical_and(z - k >= 0, can_up))
        def _():
            along_z(z - k, 1, up_sem, k).wait_send()

        @pl.when(jnp.logical_and(z + k < depth, can_down))
        def _():
            along_z(z + k, -1, down_sem, k).wait_send()

    for source in range(out_ref.shape[0]):

        @pl.when(jnp.logical_or(side != p, source != chunk))
        def _():
            pltpu.make_async_copy(out_ref.at[source], out_ref.at[source], orecv_sem.at[source]).wait()


def per_device(features, short_weight, decay_rate, residue, skip_gain, out_weight):
    lanes, rows, chans = features.shape
    groups, modes = decay_rate.shape
    width = chans // groups
    taps = short_weight.shape[1]
    count = lax.axis_size("ctx")
    tps = lax.axis_size("tp")
    me = lax.axis_index("ctx")
    cb = min(chans, 1024)
    pairs = [(i, i + 1) for i in range(count - 1)]
    if count == 16 and tps == 2:
        pair_weight = lax.ppermute(out_weight, "ctx", [(i, i ^ 1) for i in range(count)])
    rim = lax.ppermute(features[:, rows - (taps - 1) :, :], "ctx", pairs)
    rim = jnp.pad(rim, ((0, 0), (8 - (taps - 1), 0), (0, 0)))
    coef = residue * jnp.sqrt(-jnp.expm1(-2.0 * decay_rate))
    spread = (
        lax.broadcasted_iota(jnp.int32, (groups, chans), 1) // width
        == lax.broadcasted_iota(jnp.int32, (groups, chans), 0)
    ).astype(jnp.float32)
    both = jnp.concatenate([decay_rate, coef], axis=1)
    wide = jnp.einsum("gs,gc->sc", both, spread, precision=lax.Precision.HIGHEST)
    decay_wide, coef_wide = wide[:modes], wide[modes:]
    f32 = jnp.float32
    grid = (chans // cb,)
    plane = pl.BlockSpec((rows, cb), lambda i: (0, i))
    modal = pl.BlockSpec((modes, cb), lambda i: (0, i))
    q, base, own = pl.pallas_call(
        front_kernel,
        grid=grid,
        in_specs=[
            pl.BlockSpec((lanes, rows, cb), lambda i: (0, 0, i)),
            pl.BlockSpec((lanes, 8, cb), lambda i: (0, 0, i)),
            pl.BlockSpec((lanes, taps, cb), lambda i: (0, 0, i)),
            modal,
            modal,
            pl.BlockSpec((1, cb), lambda i: (0, i)),
        ],
        out_specs=[plane, plane, modal],
        out_shape=[
            jax.ShapeDtypeStruct((rows, chans), f32),
            jax.ShapeDtypeStruct((rows, chans), f32),
            jax.ShapeDtypeStruct((modes, chans), f32),
        ],
        scratch_shapes=[
            pltpu.VMEM((lanes, rows + 8, LANES), f32),
            pltpu.VMEM((rows + 8, LANES), f32),
            pltpu.VMEM((rows, LANES), f32),
        ],
        name="front",
    )(features, rim, short_weight, decay_wide, coef_wide, skip_gain[None])
    share = chans // count
    pieces = lax.all_to_all(own, "ctx", split_axis=1, concat_axis=0, tiled=True)
    mine = lax.dynamic_slice_in_dim(decay_wide, me * share, share, axis=1)
    block_decay = jnp.exp(-mine * rows)
    running = jnp.zeros((modes, share), f32)
    before = []
    for b in range(count):
        before.append(running)
        running = running * block_decay + pieces[b * modes : (b + 1) * modes]
    incoming = lax.all_to_all(
        jnp.concatenate(before, axis=0), "ctx", split_axis=0, concat_axis=1, tiled=True
    )
    cols = out_weight.shape[1]
    if count == 16 and tps == 2:
        depth = count // 4
        dma = pltpu.SemaphoreType.DMA
        vmem = pl.BlockSpec(memory_space=pltpu.VMEM)
        out = pl.pallas_call(
            finish_kernel,
            in_specs=[vmem] * 7,
            out_specs=vmem,
            out_shape=jax.ShapeDtypeStruct((count // 2, rows, cols), jnp.bfloat16),
            scratch_shapes=[
                pltpu.VMEM((2 * depth, rows, chans), jnp.bfloat16),
                pltpu.VMEM((depth, 2, 2 * rows, cols), f32),
                pltpu.VMEM((depth, 2 * rows, cols), f32),
                pltpu.VMEM((depth, 2, rows, cols), jnp.bfloat16),
                dma((depth - 1,)),
                dma((depth - 1,)),
                dma((depth,)),
                dma((depth,)),
                dma((depth,)),
                dma((depth,)),
                dma((depth,)),
                dma((depth, 2)),
                dma((count // 2,)),
            ],
            compiler_params=pltpu.CompilerParams(
                collective_id=0, has_side_effects=True, vmem_limit_bytes=40 * 1024 * 1024
            ),
            cost_estimate=pl.CostEstimate(
                flops=2 * 8 * rows * chans * 2 * cols, bytes_accessed=8 * 1024 * 1024, transcendentals=0
            ),
            name="finish",
        )(q, base, incoming, decay_wide, coef_wide, out_weight, pair_weight)
        return out.transpose(1, 0, 2).reshape(rows, count // 2 * cols)
    mixed = pl.pallas_call(
        back_kernel,
        grid=grid,
        in_specs=[plane, plane, modal, modal, modal],
        out_specs=plane,
        out_shape=jax.ShapeDtypeStruct((rows, chans), jnp.bfloat16),
        name="back",
    )(q, base, incoming, decay_wide, coef_wide)
    every = lax.all_gather(mixed, "ctx", axis=0, tiled=True)
    partial_out = jnp.dot(every, out_weight, preferred_element_type=f32)
    sums = lax.psum_scatter(partial_out, "tp", scatter_dimension=1, tiled=True).astype(jnp.bfloat16)
    turned = lax.all_to_all(sums, "ctx", split_axis=0, concat_axis=1, tiled=True)
    part = cols // tps
    swapped = lax.all_to_all(
        turned.reshape(rows, count * part), "tp", split_axis=1, concat_axis=0, tiled=True
    )
    swapped = swapped.reshape(tps, rows, count // tps, part)
    return swapped.transpose(1, 2, 0, 3).reshape(rows, count // tps * cols)


def solution(mesh):
    placed = (
        P(None, "ctx", "tp"),
        P(None, None, "tp"),
        P("tp", None),
        P("tp", None),
        P("tp"),
        P("tp", "ctx"),
    )
    return jax.shard_map(
        per_device, mesh=mesh, in_specs=placed, out_specs=P("ctx", "tp"), check_vma=False
    )
```

```python
import jax
import jax.numpy as jnp
from jax import lax
from jax.experimental import pallas as pl
from jax.experimental.pallas import tpu as pltpu
from jax.sharding import PartitionSpec as P

LANES = 128
WCUTS = 4


def modal_sum(decay, weight, rows, shift):
    modes = decay.shape[0]
    lag = lax.broadcasted_iota(jnp.int32, (8, LANES), 0).astype(jnp.float32) + shift
    total = [jnp.zeros((8, LANES), jnp.float32) for _ in range(rows // 8)]
    for s in range(modes):
        rate = decay[s : s + 1]
        power = weight[s : s + 1] * jnp.exp(-rate * lag)
        stride = jnp.exp(-8.0 * rate)
        for b in range(rows // 8):
            total[b] = total[b] + power
            if b + 1 < rows // 8:
                power = power * stride
    return total


def front_kernel(x_ref, rim_ref, w_ref, decay_ref, coef_ref, skip_ref, q_ref, base_ref, state_ref, ext, filt, gate):
    rows = x_ref.shape[1]
    taps = w_ref.shape[1]
    modes = decay_ref.shape[0]
    nb = rows // 8

    def tile(i, carry):
        at = pl.ds(pl.multiple_of(i * LANES, LANES), LANES)
        conv = []
        for lane in range(3):
            ext[lane, 0:8] = rim_ref[lane, :, at].astype(jnp.float32)
            ext[lane, 8 : 8 + rows] = x_ref[lane, :, at].astype(jnp.float32)
            acc = jnp.zeros((rows, LANES), jnp.float32)
            for j in range(taps):
                acc = acc + w_ref[lane, j : j + 1, at] * ext[lane, 8 - j : 8 - j + rows]
            conv.append(acc)
        q_ref[:, at] = conv[0]
        gated = (conv[1] * conv[2]).astype(jnp.bfloat16).astype(jnp.float32)
        gate[...] = gated
        decay = decay_ref[:, at]
        coef = coef_ref[:, at]
        filt[0:8] = jnp.zeros((8, LANES), jnp.float32)
        for b, part in enumerate(modal_sum(decay, coef, rows, 0.0)):
            filt[8 + 8 * b : 16 + 8 * b] = part.astype(jnp.bfloat16).astype(jnp.float32)
        skip = skip_ref[:, at]
        out = [skip * gated[8 * b : 8 * b + 8] for b in range(nb)]
        for t in range(rows):
            row = jnp.broadcast_to(gate[t : t + 1], (8, LANES))
            for b in range(t // 8, nb):
                start = 8 + 8 * b - t
                out[b] = out[b] + filt[start : start + 8] * row
        for b in range(nb):
            base_ref[8 * b : 8 * b + 8, at] = out[b]
        left = 7.0 - lax.broadcasted_iota(jnp.int32, (8, LANES), 0).astype(jnp.float32)
        ends = []
        for s in range(modes):
            rate = decay[s : s + 1]
            stride = jnp.exp(-8.0 * rate)
            acc = gated[0:8]
            for b in range(1, nb):
                acc = acc * stride + gated[8 * b : 8 * b + 8]
            ends.append(jnp.sum(acc * jnp.exp(-rate * left), axis=0, keepdims=True))
        state_ref[:, at] = jnp.concatenate(ends, axis=0)
        return carry

    lax.fori_loop(0, x_ref.shape[2] // LANES, tile, 0)


def back_kernel(q_ref, base_ref, state_ref, decay_ref, coef_ref, mixed_ref):
    rows = q_ref.shape[0]

    def tile(i, carry):
        at = pl.ds(pl.multiple_of(i * LANES, LANES), LANES)
        far = modal_sum(decay_ref[:, at], coef_ref[:, at] * state_ref[:, at], rows, 1.0)
        whole = jnp.concatenate(far, axis=0) + base_ref[:, at]
        mixed_ref[:, at] = (q_ref[:, at] * whole).astype(jnp.bfloat16)
        return carry

    lax.fori_loop(0, q_ref.shape[1] // LANES, tile, 0)


def finish_kernel(
    q_ref, base_ref, state_ref, decay_ref, coef_ref, own_ref, out_ref,
    blocks, result, other, packed, pair, wsend_sem, wrecv_sem,
    up_sem, down_sem, z_sem, ysend_sem, yrecv_sem, psend_sem, precv_sem, osend_sem, orecv_sem,
):
    rows = q_ref.shape[0]
    c, p = lax.axis_index("ctx"), lax.axis_index("tp")
    x, y, z = c % 2, (c // 2) % 2, c // 4
    depth = blocks.shape[0] // 2
    mesh_ids = pl.DeviceIdType.MESH
    barrier = pltpu.get_barrier_semaphore()
    for far_z in range(depth):
        for far_y in range(2):
            for far_p in range(2):
                spot = far_z * 4 + far_y * 2 + x

                @pl.when(jnp.logical_or(spot != c, p != far_p))
                def _():
                    pl.semaphore_signal(
                        barrier, inc=1, device_id=(spot, far_p), device_id_type=mesh_ids
                    )

    beside = c + 1 - 2 * x
    pl.semaphore_signal(barrier, inc=1, device_id=(beside, p), device_id_type=mesh_ids)
    here = z * 2 + y
    span = own_ref.shape[0] // WCUTS

    def weights(k):
        at = pl.ds(k * span, span)
        return pltpu.make_async_remote_copy(
            own_ref.at[at], pair.at[at], wsend_sem.at[k], wrecv_sem.at[k],
            device_id=(beside, p), device_id_type=mesh_ids,
        )

    def tile(i, carry):
        at = pl.ds(pl.multiple_of(i * LANES, LANES), LANES)
        far = modal_sum(decay_ref[:, at], coef_ref[:, at] * state_ref[:, at], rows, 1.0)
        whole = jnp.concatenate(far, axis=0) + base_ref[:, at]
        blocks[here, :, at] = (q_ref[:, at] * whole).astype(jnp.bfloat16)
        return carry

    lax.fori_loop(0, q_ref.shape[1] // LANES, tile, 0)
    pl.semaphore_wait(barrier, depth * 4)

    def along_z(level, step, sems, k):
        slot = level * 2 + y
        return pltpu.make_async_remote_copy(
            blocks.at[slot], blocks.at[slot], sems.at[k], z_sem.at[level],
            device_id=(c + 4 * step, p), device_id_type=mesh_ids,
        )

    def along_y(level):
        slot = level * 2 + y
        return pltpu.make_async_remote_copy(
            blocks.at[slot], blocks.at[slot], ysend_sem.at[level], yrecv_sem.at[level],
            device_id=(c + 2 - 4 * y, p), device_id_type=mesh_ids,
        )

    def to_core(level):
        return pltpu.make_async_remote_copy(
            result.at[level, 1 - p], other.at[level], psend_sem.at[level], precv_sem.at[level],
            device_id=(c, 1 - p), device_id_type=mesh_ids,
        )

    chunk = (c % 8) // 2 * 2 + p
    side = z // 2

    def to_owner(level, far_y):
        return pltpu.make_async_remote_copy(
            packed.at[level, far_y], out_ref.at[chunk], osend_sem.at[level, far_y], orecv_sem.at[chunk],
            device_id=(level * 4 + far_y * 2 + x, side), device_id_type=mesh_ids,
        )

    def multiply(level):
        pltpu.make_async_copy(blocks.at[level * 2 + 1 - y], blocks.at[level * 2 + 1 - y], yrecv_sem.at[level]).wait()
        lhs = blocks[pl.ds(level * 2, 2)].reshape(2 * rows, blocks.shape[2])
        result[level, x] = jnp.dot(lhs, own_ref[...], preferred_element_type=jnp.float32)

    def deliver(level):
        to_core(level).wait_recv()
        total = result[level, p] + other[level]
        packed[level] = total.astype(jnp.bfloat16).reshape(2, rows, total.shape[1])
        for far_y in range(2):
            mine = jnp.logical_and(jnp.logical_and(level == z, far_y == y), side == p)

            @pl.when(mine)
            def _():
                out_ref[chunk] = packed[level, far_y]

            @pl.when(jnp.logical_not(mine))
            def _():
                to_owner(level, far_y).start()

    def both(k, act):
        @pl.when(z - k >= 0)
        def _():
            act(z - k, 1)

        if k:

            @pl.when(z + k < depth)
            def _():
                act(z + k, -1)

    can_up, can_down = z + 1 < depth, z >= 1

    def forward(level, step, k):
        if k + 1 < depth:
            if step > 0 or k == 0:

                @pl.when(can_up)
                def _():
                    along_z(level, 1, up_sem, k).start()

            if step < 0 or k == 0:

                @pl.when(can_down)
                def _():
                    along_z(level, -1, down_sem, k).start()

        along_y(level).start()

    def arrive(k):
        def act(level, step):
            pltpu.make_async_copy(blocks.at[level * 2 + y], blocks.at[level * 2 + y], z_sem.at[level]).wait()
            forward(level, step, k)

        return act

    forward(z, 1, 0)
    for k in range(WCUTS):
        weights(k).start()
    for k in range(1, depth):
        both(k, arrive(k))
        both(k - 1, lambda level, step: multiply(level))
    both(depth - 1, lambda level, step: multiply(level))
    for k in range(WCUTS):
        weights(k).wait()
        lhs = blocks[:, :, k * span : (k + 1) * span].reshape(2 * depth * rows, span)
        term = jnp.dot(lhs, pair[k * span : (k + 1) * span], preferred_element_type=jnp.float32)
        term = term.reshape(depth, 2 * rows, term.shape[1])
        result[:, 1 - x] = term if k == 0 else result[:, 1 - x] + term
    for level in range(depth):
        to_core(level).start()
    for level in range(depth):
        deliver(level)

    for level in range(depth):
        along_y(level).wait_send()
        to_core(level).wait_send()
        for far_y in range(2):
            mine = jnp.logical_and(jnp.logical_and(level == z, far_y == y), side == p)

            @pl.when(jnp.logical_not(mine))
            def _():
                to_owner(level, far_y).wait_send()

    for k in range(depth - 1):

        @pl.when(jnp.logical_and(z - k >= 0, can_up))
        def _():
            along_z(z - k, 1, up_sem, k).wait_send()

        @pl.when(jnp.logical_and(z + k < depth, can_down))
        def _():
            along_z(z + k, -1, down_sem, k).wait_send()

    for source in range(out_ref.shape[0]):

        @pl.when(jnp.logical_or(side != p, source != chunk))
        def _():
            pltpu.make_async_copy(out_ref.at[source], out_ref.at[source], orecv_sem.at[source]).wait()


def per_device(features, short_weight, decay_rate, residue, skip_gain, out_weight):
    lanes, rows, chans = features.shape
    groups, modes = decay_rate.shape
    width = chans // groups
    taps = short_weight.shape[1]
    count = lax.axis_size("ctx")
    tps = lax.axis_size("tp")
    me = lax.axis_index("ctx")
    cb = min(chans, 1024)
    pairs = [(i, i + 1) for i in range(count - 1)]
    rim = lax.ppermute(features[:, rows - (taps - 1) :, :], "ctx", pairs)
    rim = jnp.pad(rim, ((0, 0), (8 - (taps - 1), 0), (0, 0)))
    coef = residue * jnp.sqrt(-jnp.expm1(-2.0 * decay_rate))
    spread = (
        lax.broadcasted_iota(jnp.int32, (groups, chans), 1) // width
        == lax.broadcasted_iota(jnp.int32, (groups, chans), 0)
    ).astype(jnp.float32)
    both = jnp.concatenate([decay_rate, coef], axis=1)
    wide = jnp.einsum("gs,gc->sc", both, spread, precision=lax.Precision.HIGHEST)
    decay_wide, coef_wide = wide[:modes], wide[modes:]
    f32 = jnp.float32
    grid = (chans // cb,)
    plane = pl.BlockSpec((rows, cb), lambda i: (0, i))
    modal = pl.BlockSpec((modes, cb), lambda i: (0, i))
    q, base, own = pl.pallas_call(
        front_kernel,
        grid=grid,
        in_specs=[
            pl.BlockSpec((lanes, rows, cb), lambda i: (0, 0, i)),
            pl.BlockSpec((lanes, 8, cb), lambda i: (0, 0, i)),
            pl.BlockSpec((lanes, taps, cb), lambda i: (0, 0, i)),
            modal,
            modal,
            pl.BlockSpec((1, cb), lambda i: (0, i)),
        ],
        out_specs=[plane, plane, modal],
        out_shape=[
            jax.ShapeDtypeStruct((rows, chans), f32),
            jax.ShapeDtypeStruct((rows, chans), f32),
            jax.ShapeDtypeStruct((modes, chans), f32),
        ],
        scratch_shapes=[
            pltpu.VMEM((lanes, rows + 8, LANES), f32),
            pltpu.VMEM((rows + 8, LANES), f32),
            pltpu.VMEM((rows, LANES), f32),
        ],
        name="front",
    )(features, rim, short_weight, decay_wide, coef_wide, skip_gain[None])
    share = chans // count
    pieces = lax.all_to_all(own, "ctx", split_axis=1, concat_axis=0, tiled=True)
    mine = lax.dynamic_slice_in_dim(decay_wide, me * share, share, axis=1)
    block_decay = jnp.exp(-mine * rows)
    running = jnp.zeros((modes, share), f32)
    before = []
    for b in range(count):
        before.append(running)
        running = running * block_decay + pieces[b * modes : (b + 1) * modes]
    incoming = lax.all_to_all(
        jnp.concatenate(before, axis=0), "ctx", split_axis=0, concat_axis=1, tiled=True
    )
    cols = out_weight.shape[1]
    if count == 16 and tps == 2:
        depth = count // 4
        dma = pltpu.SemaphoreType.DMA
        vmem = pl.BlockSpec(memory_space=pltpu.VMEM)
        out = pl.pallas_call(
            finish_kernel,
            in_specs=[vmem] * 6,
            out_specs=vmem,
            out_shape=jax.ShapeDtypeStruct((count // 2, rows, cols), jnp.bfloat16),
            scratch_shapes=[
                pltpu.VMEM((2 * depth, rows, chans), jnp.bfloat16),
                pltpu.VMEM((depth, 2, 2 * rows, cols), f32),
                pltpu.VMEM((depth, 2 * rows, cols), f32),
                pltpu.VMEM((depth, 2, rows, cols), jnp.bfloat16),
                pltpu.VMEM(out_weight.shape, jnp.bfloat16),
                dma((WCUTS,)),
                dma((WCUTS,)),
                dma((depth - 1,)),
                dma((depth - 1,)),
                dma((depth,)),
                dma((depth,)),
                dma((depth,)),
                dma((depth,)),
                dma((depth,)),
                dma((depth, 2)),
                dma((count // 2,)),
            ],
            compiler_params=pltpu.CompilerParams(
                collective_id=0, has_side_effects=True, vmem_limit_bytes=40 * 1024 * 1024
            ),
            cost_estimate=pl.CostEstimate(
                flops=2 * 8 * rows * chans * 2 * cols, bytes_accessed=8 * 1024 * 1024, transcendentals=0
            ),
            name="finish",
        )(q, base, incoming, decay_wide, coef_wide, out_weight)
        return out.transpose(1, 0, 2).reshape(rows, count // 2 * cols)
    mixed = pl.pallas_call(
        back_kernel,
        grid=grid,
        in_specs=[plane, plane, modal, modal, modal],
        out_specs=plane,
        out_shape=jax.ShapeDtypeStruct((rows, chans), jnp.bfloat16),
        name="back",
    )(q, base, incoming, decay_wide, coef_wide)
    every = lax.all_gather(mixed, "ctx", axis=0, tiled=True)
    partial_out = jnp.dot(every, out_weight, preferred_element_type=f32)
    sums = lax.psum_scatter(partial_out, "tp", scatter_dimension=1, tiled=True).astype(jnp.bfloat16)
    turned = lax.all_to_all(sums, "ctx", split_axis=0, concat_axis=1, tiled=True)
    part = cols // tps
    swapped = lax.all_to_all(
        turned.reshape(rows, count * part), "tp", split_axis=1, concat_axis=0, tiled=True
    )
    swapped = swapped.reshape(tps, rows, count // tps, part)
    return swapped.transpose(1, 2, 0, 3).reshape(rows, count // tps * cols)


def solution(mesh):
    placed = (
        P(None, "ctx", "tp"),
        P(None, None, "tp"),
        P("tp", None),
        P("tp", None),
        P("tp"),
        P("tp", "ctx"),
    )
    return jax.shard_map(
        per_device, mesh=mesh, in_specs=placed, out_specs=P("ctx", "tp"), check_vma=False
    )
```

```python
import jax
import jax.numpy as jnp
from jax import lax
from jax.experimental import pallas as pl
from jax.experimental.pallas import tpu as pltpu
from jax.sharding import PartitionSpec as P

LANES = 128
WCUTS = 4


def modal_sum(decay, weight, rows, shift):
    modes = decay.shape[0]
    lag = lax.broadcasted_iota(jnp.int32, (8, LANES), 0).astype(jnp.float32) + shift
    total = [jnp.zeros((8, LANES), jnp.float32) for _ in range(rows // 8)]
    for s in range(modes):
        rate = decay[s : s + 1]
        power = weight[s : s + 1] * jnp.exp(-rate * lag)
        stride = jnp.exp(-8.0 * rate)
        for b in range(rows // 8):
            total[b] = total[b] + power
            if b + 1 < rows // 8:
                power = power * stride
    return total


def front_tile(at, x_ref, rim_ref, w_ref, decay_ref, coef_ref, skip_ref, q_ref, base_ref, ext, filt, gate):
    rows = x_ref.shape[1]
    taps = w_ref.shape[1]
    modes = decay_ref.shape[0]
    nb = rows // 8

    conv = []
    for lane in range(3):
        ext[lane, 0:8] = rim_ref[lane, :, at].astype(jnp.float32)
        ext[lane, 8 : 8 + rows] = x_ref[lane, :, at].astype(jnp.float32)
        acc = jnp.zeros((rows, LANES), jnp.float32)
        for j in range(taps):
            acc = acc + w_ref[lane, j : j + 1, at] * ext[lane, 8 - j : 8 - j + rows]
        conv.append(acc)
    q_ref[:, at] = conv[0]
    gated = (conv[1] * conv[2]).astype(jnp.bfloat16).astype(jnp.float32)
    gate[...] = gated
    decay = decay_ref[:, at]
    coef = coef_ref[:, at]
    filt[0:8] = jnp.zeros((8, LANES), jnp.float32)
    for b, part in enumerate(modal_sum(decay, coef, rows, 0.0)):
        filt[8 + 8 * b : 16 + 8 * b] = part.astype(jnp.bfloat16).astype(jnp.float32)
    skip = skip_ref[:, at]
    out = [skip * gated[8 * b : 8 * b + 8] for b in range(nb)]
    for t in range(rows):
        row = jnp.broadcast_to(gate[t : t + 1], (8, LANES))
        for b in range(t // 8, nb):
            start = 8 + 8 * b - t
            out[b] = out[b] + filt[start : start + 8] * row
    for b in range(nb):
        base_ref[8 * b : 8 * b + 8, at] = out[b]
    left = 7.0 - lax.broadcasted_iota(jnp.int32, (8, LANES), 0).astype(jnp.float32)
    ends = []
    for s in range(modes):
        rate = decay[s : s + 1]
        stride = jnp.exp(-8.0 * rate)
        acc = gated[0:8]
        for b in range(1, nb):
            acc = acc * stride + gated[8 * b : 8 * b + 8]
        ends.append(jnp.sum(acc * jnp.exp(-rate * left), axis=0, keepdims=True))
    return jnp.concatenate(ends, axis=0)


def front_kernel(x_ref, rim_ref, w_ref, decay_ref, coef_ref, skip_ref, q_ref, base_ref, state_ref, ext, filt, gate):
    def tile(i, carry):
        at = pl.ds(pl.multiple_of(i * LANES, LANES), LANES)
        state_ref[:, at] = front_tile(
            at, x_ref, rim_ref, w_ref, decay_ref, coef_ref, skip_ref, q_ref, base_ref, ext, filt, gate
        )
        return carry

    lax.fori_loop(0, x_ref.shape[2] // LANES, tile, 0)


def back_kernel(q_ref, base_ref, state_ref, decay_ref, coef_ref, mixed_ref):
    rows = q_ref.shape[0]

    def tile(i, carry):
        at = pl.ds(pl.multiple_of(i * LANES, LANES), LANES)
        far = modal_sum(decay_ref[:, at], coef_ref[:, at] * state_ref[:, at], rows, 1.0)
        whole = jnp.concatenate(far, axis=0) + base_ref[:, at]
        mixed_ref[:, at] = (q_ref[:, at] * whole).astype(jnp.bfloat16)
        return carry

    lax.fori_loop(0, q_ref.shape[1] // LANES, tile, 0)


def finish_kernel(
    x_ref, rim_ref, w_ref, decay_ref, coef_ref, skip_ref, own_ref, out_ref,
    q_ref, base_ref, ext, filt, gate, ends, gathered, ready, incoming,
    send1_sem, recv1_sem, send2_sem, recv2_sem,
    blocks, result, other, packed, pair, wsend_sem, wrecv_sem,
    up_sem, down_sem, z_sem, ysend_sem, yrecv_sem, psend_sem, precv_sem, osend_sem, orecv_sem,
):
    rows = q_ref.shape[0]
    count, modes, share = ends.shape
    c, p = lax.axis_index("ctx"), lax.axis_index("tp")
    x, y, z = c % 2, (c // 2) % 2, c // 4
    depth = blocks.shape[0] // 2
    mesh_ids = pl.DeviceIdType.MESH
    barrier = pltpu.get_barrier_semaphore()
    for spot in range(count):

        @pl.when(spot != c)
        def _():
            pl.semaphore_signal(barrier, inc=1, device_id=(spot, p), device_id_type=mesh_ids)

    for far in range(2 * depth):
        pl.semaphore_signal(barrier, inc=1, device_id=(far * 2 + x, 1 - p), device_id_type=mesh_ids)
    pl.semaphore_wait(barrier, count - 1 + 2 * depth)
    beside = c + 1 - 2 * x
    here = z * 2 + y
    span = own_ref.shape[0] // WCUTS

    def weights(k):
        at = pl.ds(k * span, span)
        return pltpu.make_async_remote_copy(
            own_ref.at[at], pair.at[at], wsend_sem.at[k], wrecv_sem.at[k],
            device_id=(beside, p), device_id_type=mesh_ids,
        )

    halves = share // LANES

    def hand_over(d):
        return pltpu.make_async_remote_copy(
            ends.at[d], gathered.at[c], send1_sem.at[d], recv1_sem.at[c],
            device_id=(d, p), device_id_type=mesh_ids,
        )

    def hand_back(d):
        return pltpu.make_async_remote_copy(
            ready.at[d], incoming.at[c], send2_sem.at[d], recv2_sem.at[c],
            device_id=(d, p), device_id_type=mesh_ids,
        )

    def landed(buf, sems, d):
        pltpu.make_async_copy(buf.at[d], buf.at[d], sems.at[d]).wait()

    def front_step(j, carry):
        d = lax.rem(c + 1 + j, count)
        for h in range(halves):
            at = pl.ds(pl.multiple_of(d * share + h * LANES, LANES), LANES)
            ends[d, :, h * LANES : (h + 1) * LANES] = front_tile(
                at, x_ref, rim_ref, w_ref, decay_ref, coef_ref, skip_ref, q_ref, base_ref, ext, filt, gate
            )

        @pl.when(d != c)
        def _():
            hand_over(d).start()

        return carry

    lax.fori_loop(0, count, front_step, 0)
    gathered[c] = ends[c]
    mine = decay_ref[:, pl.ds(pl.multiple_of(c * share, LANES), share)]
    block_decay = jnp.exp(-mine * rows)
    running = jnp.zeros((modes, share), jnp.float32)
    for d in range(count):
        ready[d] = running

        @pl.when(d != c)
        def _():
            hand_back(d).start()
            landed(gathered, recv1_sem, d)

        running = running * block_decay + gathered[d]
    incoming[c] = ready[c]
    for d in range(count):

        @pl.when(d != c)
        def _():
            hand_over(d).wait_send()
            hand_back(d).wait_send()
            landed(incoming, recv2_sem, d)

    for k in range(WCUTS):
        weights(k).start()

    def back_step(d, carry):
        for h in range(halves):
            at = pl.ds(pl.multiple_of(d * share + h * LANES, LANES), LANES)
            state = incoming[d, :, h * LANES : (h + 1) * LANES]
            far = modal_sum(decay_ref[:, at], coef_ref[:, at] * state, rows, 1.0)
            whole = jnp.concatenate(far, axis=0) + base_ref[:, at]
            blocks[here, :, at] = (q_ref[:, at] * whole).astype(jnp.bfloat16)
        return carry

    lax.fori_loop(0, count, back_step, 0)

    def along_z(level, step, sems, k):
        slot = level * 2 + y
        return pltpu.make_async_remote_copy(
            blocks.at[slot], blocks.at[slot], sems.at[k], z_sem.at[level],
            device_id=(c + 4 * step, p), device_id_type=mesh_ids,
        )

    def along_y(level):
        slot = level * 2 + y
        return pltpu.make_async_remote_copy(
            blocks.at[slot], blocks.at[slot], ysend_sem.at[level], yrecv_sem.at[level],
            device_id=(c + 2 - 4 * y, p), device_id_type=mesh_ids,
        )

    def to_core(level):
        return pltpu.make_async_remote_copy(
            result.at[level, 1 - p], other.at[level], psend_sem.at[level], precv_sem.at[level],
            device_id=(c, 1 - p), device_id_type=mesh_ids,
        )

    chunk = (c % 8) // 2 * 2 + p
    side = z // 2

    def to_owner(level, far_y):
        return pltpu.make_async_remote_copy(
            packed.at[level, far_y], out_ref.at[chunk], osend_sem.at[level, far_y], orecv_sem.at[chunk],
            device_id=(level * 4 + far_y * 2 + x, side), device_id_type=mesh_ids,
        )

    def multiply(level):
        pltpu.make_async_copy(blocks.at[level * 2 + 1 - y], blocks.at[level * 2 + 1 - y], yrecv_sem.at[level]).wait()
        lhs = blocks[pl.ds(level * 2, 2)].reshape(2 * rows, blocks.shape[2])
        result[level, x] = jnp.dot(lhs, own_ref[...], preferred_element_type=jnp.float32)

    def deliver(level):
        to_core(level).wait_recv()
        total = result[level, p] + other[level]
        packed[level] = total.astype(jnp.bfloat16).reshape(2, rows, total.shape[1])
        for far_y in range(2):
            mine = jnp.logical_and(jnp.logical_and(level == z, far_y == y), side == p)

            @pl.when(mine)
            def _():
                out_ref[chunk] = packed[level, far_y]

            @pl.when(jnp.logical_not(mine))
            def _():
                to_owner(level, far_y).start()

    def both(k, act):
        @pl.when(z - k >= 0)
        def _():
            act(z - k, 1)

        if k:

            @pl.when(z + k < depth)
            def _():
                act(z + k, -1)

    can_up, can_down = z + 1 < depth, z >= 1

    def forward(level, step, k):
        if k + 1 < depth:
            if step > 0 or k == 0:

                @pl.when(can_up)
                def _():
                    along_z(level, 1, up_sem, k).start()

            if step < 0 or k == 0:

                @pl.when(can_down)
                def _():
                    along_z(level, -1, down_sem, k).start()

        along_y(level).start()

    def arrive(k):
        def act(level, step):
            pltpu.make_async_copy(blocks.at[level * 2 + y], blocks.at[level * 2 + y], z_sem.at[level]).wait()
            forward(level, step, k)

        return act

    forward(z, 1, 0)
    for k in range(1, depth):
        both(k, arrive(k))
        both(k - 1, lambda level, step: multiply(level))
    both(depth - 1, lambda level, step: multiply(level))
    for k in range(WCUTS):
        weights(k).wait()
        lhs = blocks[:, :, k * span : (k + 1) * span].reshape(2 * depth * rows, span)
        term = jnp.dot(lhs, pair[k * span : (k + 1) * span], preferred_element_type=jnp.float32)
        term = term.reshape(depth, 2 * rows, term.shape[1])
        result[:, 1 - x] = term if k == 0 else result[:, 1 - x] + term
    for level in range(depth):
        to_core(level).start()
    for level in range(depth):
        deliver(level)

    for level in range(depth):
        along_y(level).wait_send()
        to_core(level).wait_send()
        for far_y in range(2):
            mine = jnp.logical_and(jnp.logical_and(level == z, far_y == y), side == p)

            @pl.when(jnp.logical_not(mine))
            def _():
                to_owner(level, far_y).wait_send()

    for k in range(depth - 1):

        @pl.when(jnp.logical_and(z - k >= 0, can_up))
        def _():
            along_z(z - k, 1, up_sem, k).wait_send()

        @pl.when(jnp.logical_and(z + k < depth, can_down))
        def _():
            along_z(z + k, -1, down_sem, k).wait_send()

    for source in range(out_ref.shape[0]):

        @pl.when(jnp.logical_or(side != p, source != chunk))
        def _():
            pltpu.make_async_copy(out_ref.at[source], out_ref.at[source], orecv_sem.at[source]).wait()


def per_device(features, short_weight, decay_rate, residue, skip_gain, out_weight):
    lanes, rows, chans = features.shape
    groups, modes = decay_rate.shape
    width = chans // groups
    taps = short_weight.shape[1]
    count = lax.axis_size("ctx")
    tps = lax.axis_size("tp")
    me = lax.axis_index("ctx")
    cb = min(chans, 1024)
    pairs = [(i, i + 1) for i in range(count - 1)]
    rim = lax.ppermute(features[:, rows - (taps - 1) :, :], "ctx", pairs)
    rim = jnp.pad(rim, ((0, 0), (8 - (taps - 1), 0), (0, 0)))
    coef = residue * jnp.sqrt(-jnp.expm1(-2.0 * decay_rate))
    spread = (
        lax.broadcasted_iota(jnp.int32, (groups, chans), 1) // width
        == lax.broadcasted_iota(jnp.int32, (groups, chans), 0)
    ).astype(jnp.float32)
    both = jnp.concatenate([decay_rate, coef], axis=1)
    wide = jnp.einsum("gs,gc->sc", both, spread, precision=lax.Precision.HIGHEST)
    decay_wide, coef_wide = wide[:modes], wide[modes:]
    f32 = jnp.float32
    cols = out_weight.shape[1]
    if count == 16 and tps == 2:
        depth = count // 4
        dma = pltpu.SemaphoreType.DMA
        vmem = pl.BlockSpec(memory_space=pltpu.VMEM)
        out = pl.pallas_call(
            finish_kernel,
            in_specs=[vmem] * 7,
            out_specs=vmem,
            out_shape=jax.ShapeDtypeStruct((count // 2, rows, cols), jnp.bfloat16),
            scratch_shapes=[
                pltpu.VMEM((rows, chans), f32),
                pltpu.VMEM((rows, chans), f32),
                pltpu.VMEM((lanes, rows + 8, LANES), f32),
                pltpu.VMEM((rows + 8, LANES), f32),
                pltpu.VMEM((rows, LANES), f32),
                *[pltpu.VMEM((count, modes, chans // count), f32) for _ in range(4)],
                *[dma((count,)) for _ in range(4)],
                pltpu.VMEM((2 * depth, rows, chans), jnp.bfloat16),
                pltpu.VMEM((depth, 2, 2 * rows, cols), f32),
                pltpu.VMEM((depth, 2 * rows, cols), f32),
                pltpu.VMEM((depth, 2, rows, cols), jnp.bfloat16),
                pltpu.VMEM(out_weight.shape, jnp.bfloat16),
                dma((WCUTS,)),
                dma((WCUTS,)),
                dma((depth - 1,)),
                dma((depth - 1,)),
                dma((depth,)),
                dma((depth,)),
                dma((depth,)),
                dma((depth,)),
                dma((depth,)),
                dma((depth, 2)),
                dma((count // 2,)),
            ],
            compiler_params=pltpu.CompilerParams(
                collective_id=0, has_side_effects=True, vmem_limit_bytes=40 * 1024 * 1024
            ),
            cost_estimate=pl.CostEstimate(
                flops=2 * 8 * rows * chans * 2 * cols, bytes_accessed=8 * 1024 * 1024, transcendentals=0
            ),
            name="finish",
        )(features, rim, short_weight, decay_wide, coef_wide, skip_gain[None], out_weight)
        return out.transpose(1, 0, 2).reshape(rows, count // 2 * cols)
    grid = (chans // cb,)
    plane = pl.BlockSpec((rows, cb), lambda i: (0, i))
    modal = pl.BlockSpec((modes, cb), lambda i: (0, i))
    q, base, own = pl.pallas_call(
        front_kernel,
        grid=grid,
        in_specs=[
            pl.BlockSpec((lanes, rows, cb), lambda i: (0, 0, i)),
            pl.BlockSpec((lanes, 8, cb), lambda i: (0, 0, i)),
            pl.BlockSpec((lanes, taps, cb), lambda i: (0, 0, i)),
            modal,
            modal,
            pl.BlockSpec((1, cb), lambda i: (0, i)),
        ],
        out_specs=[plane, plane, modal],
        out_shape=[
            jax.ShapeDtypeStruct((rows, chans), f32),
            jax.ShapeDtypeStruct((rows, chans), f32),
            jax.ShapeDtypeStruct((modes, chans), f32),
        ],
        scratch_shapes=[
            pltpu.VMEM((lanes, rows + 8, LANES), f32),
            pltpu.VMEM((rows + 8, LANES), f32),
            pltpu.VMEM((rows, LANES), f32),
        ],
        name="front",
    )(features, rim, short_weight, decay_wide, coef_wide, skip_gain[None])
    share = chans // count
    pieces = lax.all_to_all(own, "ctx", split_axis=1, concat_axis=0, tiled=True)
    mine = lax.dynamic_slice_in_dim(decay_wide, me * share, share, axis=1)
    block_decay = jnp.exp(-mine * rows)
    running = jnp.zeros((modes, share), f32)
    before = []
    for b in range(count):
        before.append(running)
        running = running * block_decay + pieces[b * modes : (b + 1) * modes]
    incoming = lax.all_to_all(
        jnp.concatenate(before, axis=0), "ctx", split_axis=0, concat_axis=1, tiled=True
    )
    mixed = pl.pallas_call(
        back_kernel,
        grid=grid,
        in_specs=[plane, plane, modal, modal, modal],
        out_specs=plane,
        out_shape=jax.ShapeDtypeStruct((rows, chans), jnp.bfloat16),
        name="back",
    )(q, base, incoming, decay_wide, coef_wide)
    every = lax.all_gather(mixed, "ctx", axis=0, tiled=True)
    partial_out = jnp.dot(every, out_weight, preferred_element_type=f32)
    sums = lax.psum_scatter(partial_out, "tp", scatter_dimension=1, tiled=True).astype(jnp.bfloat16)
    turned = lax.all_to_all(sums, "ctx", split_axis=0, concat_axis=1, tiled=True)
    part = cols // tps
    swapped = lax.all_to_all(
        turned.reshape(rows, count * part), "tp", split_axis=1, concat_axis=0, tiled=True
    )
    swapped = swapped.reshape(tps, rows, count // tps, part)
    return swapped.transpose(1, 2, 0, 3).reshape(rows, count // tps * cols)


def solution(mesh):
    placed = (
        P(None, "ctx", "tp"),
        P(None, None, "tp"),
        P("tp", None),
        P("tp", None),
        P("tp"),
        P("tp", "ctx"),
    )
    return jax.shard_map(
        per_device, mesh=mesh, in_specs=placed, out_specs=P("ctx", "tp"), check_vma=False
    )
```

```python
import jax
import jax.numpy as jnp
from jax import lax
from jax.experimental import pallas as pl
from jax.experimental.pallas import tpu as pltpu
from jax.sharding import PartitionSpec as P

LANES = 128
WCUTS = 4
PARTS = 2


def modal_sum(decay, weight, rows, shift):
    modes = decay.shape[0]
    lag = lax.broadcasted_iota(jnp.int32, (8, LANES), 0).astype(jnp.float32) + shift
    total = [jnp.zeros((8, LANES), jnp.float32) for _ in range(rows // 8)]
    for s in range(modes):
        rate = decay[s : s + 1]
        power = weight[s : s + 1] * jnp.exp(-rate * lag)
        stride = jnp.exp(-8.0 * rate)
        for b in range(rows // 8):
            total[b] = total[b] + power
            if b + 1 < rows // 8:
                power = power * stride
    return total


def front_tile(at, x_ref, rim_ref, w_ref, decay_ref, coef_ref, skip_ref, q_ref, base_ref, ext, filt, gate):
    rows = x_ref.shape[1]
    taps = w_ref.shape[1]
    modes = decay_ref.shape[0]
    nb = rows // 8

    conv = []
    for lane in range(3):
        ext[lane, 0:8] = rim_ref[lane, :, at].astype(jnp.float32)
        ext[lane, 8 : 8 + rows] = x_ref[lane, :, at].astype(jnp.float32)
        acc = jnp.zeros((rows, LANES), jnp.float32)
        for j in range(taps):
            acc = acc + w_ref[lane, j : j + 1, at] * ext[lane, 8 - j : 8 - j + rows]
        conv.append(acc)
    q_ref[:, at] = conv[0]
    gated = (conv[1] * conv[2]).astype(jnp.bfloat16).astype(jnp.float32)
    gate[...] = gated
    decay = decay_ref[:, at]
    coef = coef_ref[:, at]
    filt[0:8] = jnp.zeros((8, LANES), jnp.float32)
    for b, part in enumerate(modal_sum(decay, coef, rows, 0.0)):
        filt[8 + 8 * b : 16 + 8 * b] = part.astype(jnp.bfloat16).astype(jnp.float32)
    skip = skip_ref[:, at]
    out = [skip * gated[8 * b : 8 * b + 8] for b in range(nb)]
    for t in range(rows):
        row = jnp.broadcast_to(gate[t : t + 1], (8, LANES))
        for b in range(t // 8, nb):
            start = 8 + 8 * b - t
            out[b] = out[b] + filt[start : start + 8] * row
    for b in range(nb):
        base_ref[8 * b : 8 * b + 8, at] = out[b]
    left = 7.0 - lax.broadcasted_iota(jnp.int32, (8, LANES), 0).astype(jnp.float32)
    ends = []
    for s in range(modes):
        rate = decay[s : s + 1]
        stride = jnp.exp(-8.0 * rate)
        acc = gated[0:8]
        for b in range(1, nb):
            acc = acc * stride + gated[8 * b : 8 * b + 8]
        ends.append(jnp.sum(acc * jnp.exp(-rate * left), axis=0, keepdims=True))
    return jnp.concatenate(ends, axis=0)


def front_kernel(x_ref, rim_ref, w_ref, decay_ref, coef_ref, skip_ref, q_ref, base_ref, state_ref, ext, filt, gate):
    def tile(i, carry):
        at = pl.ds(pl.multiple_of(i * LANES, LANES), LANES)
        state_ref[:, at] = front_tile(
            at, x_ref, rim_ref, w_ref, decay_ref, coef_ref, skip_ref, q_ref, base_ref, ext, filt, gate
        )
        return carry

    lax.fori_loop(0, x_ref.shape[2] // LANES, tile, 0)


def back_kernel(q_ref, base_ref, state_ref, decay_ref, coef_ref, mixed_ref):
    rows = q_ref.shape[0]

    def tile(i, carry):
        at = pl.ds(pl.multiple_of(i * LANES, LANES), LANES)
        far = modal_sum(decay_ref[:, at], coef_ref[:, at] * state_ref[:, at], rows, 1.0)
        whole = jnp.concatenate(far, axis=0) + base_ref[:, at]
        mixed_ref[:, at] = (q_ref[:, at] * whole).astype(jnp.bfloat16)
        return carry

    lax.fori_loop(0, q_ref.shape[1] // LANES, tile, 0)


def finish_kernel(
    x_ref, rim_ref, w_ref, decay_ref, coef_ref, skip_ref, own_ref, out_ref,
    q_ref, base_ref, ext, filt, gate, ends, gathered, ready, incoming,
    send1_sem, recv1_sem, send2_sem, recv2_sem,
    blocks, result, other, packed, pair, wsend_sem, wrecv_sem,
    up_sem, down_sem, z_sem, ysend_sem, yrecv_sem, psend_sem, precv_sem, osend_sem, orecv_sem,
):
    rows = q_ref.shape[0]
    count, modes, share = ends.shape
    c, p = lax.axis_index("ctx"), lax.axis_index("tp")
    x, y, z = c % 2, (c // 2) % 2, c // 4
    depth = blocks.shape[0] // 2
    mesh_ids = pl.DeviceIdType.MESH
    barrier = pltpu.get_barrier_semaphore()
    for spot in range(count):

        @pl.when(spot != c)
        def _():
            pl.semaphore_signal(barrier, inc=1, device_id=(spot, p), device_id_type=mesh_ids)

    for far in range(2 * depth):
        pl.semaphore_signal(barrier, inc=1, device_id=(far * 2 + x, 1 - p), device_id_type=mesh_ids)
    pl.semaphore_wait(barrier, count - 1 + 2 * depth)
    beside = c + 1 - 2 * x
    here = z * 2 + y
    span = own_ref.shape[0] // WCUTS

    def weights(k):
        at = pl.ds(k * span, span)
        return pltpu.make_async_remote_copy(
            own_ref.at[at], pair.at[at], wsend_sem.at[k], wrecv_sem.at[k],
            device_id=(beside, p), device_id_type=mesh_ids,
        )

    halves = share // LANES

    def hand_over(d):
        return pltpu.make_async_remote_copy(
            ends.at[d], gathered.at[c], send1_sem.at[d], recv1_sem.at[c],
            device_id=(d, p), device_id_type=mesh_ids,
        )

    def hand_back(d):
        return pltpu.make_async_remote_copy(
            ready.at[d], incoming.at[c], send2_sem.at[d], recv2_sem.at[c],
            device_id=(d, p), device_id_type=mesh_ids,
        )

    def landed(buf, sems, d):
        pltpu.make_async_copy(buf.at[d], buf.at[d], sems.at[d]).wait()

    def front_step(j, carry):
        d = lax.rem(c + 1 + j, count)
        for h in range(halves):
            at = pl.ds(pl.multiple_of(d * share + h * LANES, LANES), LANES)
            ends[d, :, h * LANES : (h + 1) * LANES] = front_tile(
                at, x_ref, rim_ref, w_ref, decay_ref, coef_ref, skip_ref, q_ref, base_ref, ext, filt, gate
            )

        @pl.when(d != c)
        def _():
            hand_over(d).start()

        return carry

    weights(0).start()
    lax.fori_loop(0, count, front_step, 0)
    gathered[c] = ends[c]
    mine = decay_ref[:, pl.ds(pl.multiple_of(c * share, LANES), share)]
    block_decay = jnp.exp(-mine * rows)
    running = jnp.zeros((modes, share), jnp.float32)
    for d in range(count):
        ready[d] = running

        @pl.when(d != c)
        def _():
            hand_back(d).start()
            landed(gathered, recv1_sem, d)

        running = running * block_decay + gathered[d]
    incoming[c] = ready[c]
    for d in range(count):

        @pl.when(d != c)
        def _():
            hand_over(d).wait_send()
            hand_back(d).wait_send()
            landed(incoming, recv2_sem, d)

    for k in range(1, WCUTS):
        weights(k).start()

    def back_step(d, carry):
        for h in range(halves):
            at = pl.ds(pl.multiple_of(d * share + h * LANES, LANES), LANES)
            state = incoming[d, :, h * LANES : (h + 1) * LANES]
            far = modal_sum(decay_ref[:, at], coef_ref[:, at] * state, rows, 1.0)
            whole = jnp.concatenate(far, axis=0) + base_ref[:, at]
            blocks[here, :, at] = (q_ref[:, at] * whole).astype(jnp.bfloat16)
        return carry

    part_lanes = blocks.shape[2] // PARTS

    def piece(slot, h):
        return blocks.at[slot, :, pl.ds(h * part_lanes, part_lanes)]

    def along_z(level, step, sems, k, h):
        part = piece(level * 2 + y, h)
        return pltpu.make_async_remote_copy(
            part, part, sems.at[k, h], z_sem.at[level, h],
            device_id=(c + 4 * step, p), device_id_type=mesh_ids,
        )

    def along_y(level, h):
        part = piece(level * 2 + y, h)
        return pltpu.make_async_remote_copy(
            part, part, ysend_sem.at[level, h], yrecv_sem.at[level, h],
            device_id=(c + 2 - 4 * y, p), device_id_type=mesh_ids,
        )

    def to_core(level):
        return pltpu.make_async_remote_copy(
            result.at[level, 1 - p], other.at[level], psend_sem.at[level], precv_sem.at[level],
            device_id=(c, 1 - p), device_id_type=mesh_ids,
        )

    chunk = (c % 8) // 2 * 2 + p
    side = z // 2

    def to_owner(level, far_y):
        return pltpu.make_async_remote_copy(
            packed.at[level, far_y], out_ref.at[chunk], osend_sem.at[level, far_y], orecv_sem.at[chunk],
            device_id=(level * 4 + far_y * 2 + x, side), device_id_type=mesh_ids,
        )

    def multiply(level):
        for h in range(PARTS):
            part = piece(level * 2 + 1 - y, h)
            pltpu.make_async_copy(part, part, yrecv_sem.at[level, h]).wait()
        lhs = blocks[pl.ds(level * 2, 2)].reshape(2 * rows, blocks.shape[2])
        result[level, x] = jnp.dot(lhs, own_ref[...], preferred_element_type=jnp.float32)

    def multiply_pair(level):
        lhs = blocks[pl.ds(level * 2, 2)].reshape(2 * rows, blocks.shape[2])
        result[level, 1 - x] = jnp.dot(lhs, pair[...], preferred_element_type=jnp.float32)
        to_core(level).start()

    def deliver(level):
        to_core(level).wait_recv()
        total = result[level, p] + other[level]
        packed[level] = total.astype(jnp.bfloat16).reshape(2, rows, total.shape[1])
        for far_y in range(2):
            mine = jnp.logical_and(jnp.logical_and(level == z, far_y == y), side == p)

            @pl.when(mine)
            def _():
                out_ref[chunk] = packed[level, far_y]

            @pl.when(jnp.logical_not(mine))
            def _():
                to_owner(level, far_y).start()

    def both(k, act):
        @pl.when(z - k >= 0)
        def _():
            act(z - k, 1)

        if k:

            @pl.when(z + k < depth)
            def _():
                act(z + k, -1)

    can_up, can_down = z + 1 < depth, z >= 1

    def forward(level, step, k, h):
        if k + 1 < depth:
            if step > 0 or k == 0:

                @pl.when(can_up)
                def _():
                    along_z(level, 1, up_sem, k, h).start()

            if step < 0 or k == 0:

                @pl.when(can_down)
                def _():
                    along_z(level, -1, down_sem, k, h).start()

        along_y(level, h).start()

    def arrive(k):
        def act(level, step):
            for h in range(PARTS):
                part = piece(level * 2 + y, h)
                pltpu.make_async_copy(part, part, z_sem.at[level, h]).wait()
                forward(level, step, k, h)

        return act

    per = count // PARTS
    for h in range(PARTS):
        lax.fori_loop(h * per, (h + 1) * per, back_step, 0)
        forward(z, 1, 0, h)
    for k in range(1, depth):
        both(k, arrive(k))
        if k == depth - 1:
            for j in range(WCUTS):
                weights(j).wait()
            for j in range(k - 1):
                both(j, lambda level, step: multiply_pair(level))
        both(k - 1, lambda level, step: multiply(level))
        if k == depth - 1:
            both(k - 1, lambda level, step: multiply_pair(level))
            for j in range(k - 1):
                both(j, lambda level, step: deliver(level))
    both(depth - 1, lambda level, step: multiply(level))
    both(depth - 1, lambda level, step: multiply_pair(level))
    both(depth - 2, lambda level, step: deliver(level))
    both(depth - 1, lambda level, step: deliver(level))

    for level in range(depth):
        for h in range(PARTS):
            along_y(level, h).wait_send()
        to_core(level).wait_send()
        for far_y in range(2):
            mine = jnp.logical_and(jnp.logical_and(level == z, far_y == y), side == p)

            @pl.when(jnp.logical_not(mine))
            def _():
                to_owner(level, far_y).wait_send()

    for k in range(depth - 1):

        @pl.when(jnp.logical_and(z - k >= 0, can_up))
        def _():
            for h in range(PARTS):
                along_z(z - k, 1, up_sem, k, h).wait_send()

        @pl.when(jnp.logical_and(z + k < depth, can_down))
        def _():
            for h in range(PARTS):
                along_z(z + k, -1, down_sem, k, h).wait_send()

    for source in range(out_ref.shape[0]):

        @pl.when(jnp.logical_or(side != p, source != chunk))
        def _():
            pltpu.make_async_copy(out_ref.at[source], out_ref.at[source], orecv_sem.at[source]).wait()


def per_device(features, short_weight, decay_rate, residue, skip_gain, out_weight):
    lanes, rows, chans = features.shape
    groups, modes = decay_rate.shape
    width = chans // groups
    taps = short_weight.shape[1]
    count = lax.axis_size("ctx")
    tps = lax.axis_size("tp")
    me = lax.axis_index("ctx")
    cb = min(chans, 1024)
    pairs = [(i, i + 1) for i in range(count - 1)]
    rim = lax.ppermute(features[:, rows - (taps - 1) :, :], "ctx", pairs)
    rim = jnp.pad(rim, ((0, 0), (8 - (taps - 1), 0), (0, 0)))
    coef = residue * jnp.sqrt(-jnp.expm1(-2.0 * decay_rate))
    spread = (
        lax.broadcasted_iota(jnp.int32, (groups, chans), 1) // width
        == lax.broadcasted_iota(jnp.int32, (groups, chans), 0)
    ).astype(jnp.float32)
    both = jnp.concatenate([decay_rate, coef], axis=1)
    wide = jnp.einsum("gs,gc->sc", both, spread, precision=lax.Precision.HIGHEST)
    decay_wide, coef_wide = wide[:modes], wide[modes:]
    f32 = jnp.float32
    cols = out_weight.shape[1]
    if count == 16 and tps == 2:
        depth = count // 4
        dma = pltpu.SemaphoreType.DMA
        vmem = pl.BlockSpec(memory_space=pltpu.VMEM)
        out = pl.pallas_call(
            finish_kernel,
            in_specs=[vmem] * 7,
            out_specs=vmem,
            out_shape=jax.ShapeDtypeStruct((count // 2, rows, cols), jnp.bfloat16),
            scratch_shapes=[
                pltpu.VMEM((rows, chans), f32),
                pltpu.VMEM((rows, chans), f32),
                pltpu.VMEM((lanes, rows + 8, LANES), f32),
                pltpu.VMEM((rows + 8, LANES), f32),
                pltpu.VMEM((rows, LANES), f32),
                *[pltpu.VMEM((count, modes, chans // count), f32) for _ in range(4)],
                *[dma((count,)) for _ in range(4)],
                pltpu.VMEM((2 * depth, rows, chans), jnp.bfloat16),
                pltpu.VMEM((depth, 2, 2 * rows, cols), f32),
                pltpu.VMEM((depth, 2 * rows, cols), f32),
                pltpu.VMEM((depth, 2, rows, cols), jnp.bfloat16),
                pltpu.VMEM(out_weight.shape, jnp.bfloat16),
                dma((WCUTS,)),
                dma((WCUTS,)),
                dma((depth - 1, PARTS)),
                dma((depth - 1, PARTS)),
                dma((depth, PARTS)),
                dma((depth, PARTS)),
                dma((depth, PARTS)),
                dma((depth,)),
                dma((depth,)),
                dma((depth, 2)),
                dma((count // 2,)),
            ],
            compiler_params=pltpu.CompilerParams(
                collective_id=0, has_side_effects=True, vmem_limit_bytes=40 * 1024 * 1024
            ),
            cost_estimate=pl.CostEstimate(
                flops=2 * 8 * rows * chans * 2 * cols, bytes_accessed=8 * 1024 * 1024, transcendentals=0
            ),
            name="finish",
        )(features, rim, short_weight, decay_wide, coef_wide, skip_gain[None], out_weight)
        return out.transpose(1, 0, 2).reshape(rows, count // 2 * cols)
    grid = (chans // cb,)
    plane = pl.BlockSpec((rows, cb), lambda i: (0, i))
    modal = pl.BlockSpec((modes, cb), lambda i: (0, i))
    q, base, own = pl.pallas_call(
        front_kernel,
        grid=grid,
        in_specs=[
            pl.BlockSpec((lanes, rows, cb), lambda i: (0, 0, i)),
            pl.BlockSpec((lanes, 8, cb), lambda i: (0, 0, i)),
            pl.BlockSpec((lanes, taps, cb), lambda i: (0, 0, i)),
            modal,
            modal,
            pl.BlockSpec((1, cb), lambda i: (0, i)),
        ],
        out_specs=[plane, plane, modal],
        out_shape=[
            jax.ShapeDtypeStruct((rows, chans), f32),
            jax.ShapeDtypeStruct((rows, chans), f32),
            jax.ShapeDtypeStruct((modes, chans), f32),
        ],
        scratch_shapes=[
            pltpu.VMEM((lanes, rows + 8, LANES), f32),
            pltpu.VMEM((rows + 8, LANES), f32),
            pltpu.VMEM((rows, LANES), f32),
        ],
        name="front",
    )(features, rim, short_weight, decay_wide, coef_wide, skip_gain[None])
    share = chans // count
    pieces = lax.all_to_all(own, "ctx", split_axis=1, concat_axis=0, tiled=True)
    mine = lax.dynamic_slice_in_dim(decay_wide, me * share, share, axis=1)
    block_decay = jnp.exp(-mine * rows)
    running = jnp.zeros((modes, share), f32)
    before = []
    for b in range(count):
        before.append(running)
        running = running * block_decay + pieces[b * modes : (b + 1) * modes]
    incoming = lax.all_to_all(
        jnp.concatenate(before, axis=0), "ctx", split_axis=0, concat_axis=1, tiled=True
    )
    mixed = pl.pallas_call(
        back_kernel,
        grid=grid,
        in_specs=[plane, plane, modal, modal, modal],
        out_specs=plane,
        out_shape=jax.ShapeDtypeStruct((rows, chans), jnp.bfloat16),
        name="back",
    )(q, base, incoming, decay_wide, coef_wide)
    every = lax.all_gather(mixed, "ctx", axis=0, tiled=True)
    partial_out = jnp.dot(every, out_weight, preferred_element_type=f32)
    sums = lax.psum_scatter(partial_out, "tp", scatter_dimension=1, tiled=True).astype(jnp.bfloat16)
    turned = lax.all_to_all(sums, "ctx", split_axis=0, concat_axis=1, tiled=True)
    part = cols // tps
    swapped = lax.all_to_all(
        turned.reshape(rows, count * part), "tp", split_axis=1, concat_axis=0, tiled=True
    )
    swapped = swapped.reshape(tps, rows, count // tps, part)
    return swapped.transpose(1, 2, 0, 3).reshape(rows, count // tps * cols)


def solution(mesh):
    placed = (
        P(None, "ctx", "tp"),
        P(None, None, "tp"),
        P("tp", None),
        P("tp", None),
        P("tp"),
        P("tp", "ctx"),
    )
    return jax.shard_map(
        per_device, mesh=mesh, in_specs=placed, out_specs=P("ctx", "tp"), check_vma=False
    )
```
